768 devices in a mesh: blk: 32 (over y_hi, x, core), rep: 24 (over y_lo, z).
Axes of the slice: x: 4, y: 8 (y_hi: 4, y_lo: 2; y = y_hi * 2 + y_lo), z: 12, core: 2. Of those that a mesh axis runs over, the one named last changes fastest.
Arguments:
- features: bfloat16 [98304, 128], P(('blk', 'rep')), may hold values from -6 to 6
- w_self: bfloat16 [128, 256], replicated, may hold values from -0.5 to 0.5
- w_neigh: bfloat16 [128, 256], replicated, may hold values from -0.5 to 0.5
- cotangent: bfloat16 [98304, 256], P(('blk', 'rep')), may hold values from -6 to 6
- tile_values: bfloat16 [32, 24, 96, 128, 128], P('blk', 'rep'), may hold values from -0.0546875 to 0.0546875
- tile_row: int32 [32, 24, 96], P('blk', 'rep'), may hold values from 0 to 31
- tile_col: int32 [32, 24, 96], P('blk', 'rep'), may hold values from 0 to 23
- tile_count: int32 [32, 24, 96], P('blk', 'rep'), may hold values from 0 to 16384, as said below
Outputs:
- activated: bfloat16 [98304, 256], P(('blk', 'rep'))
- input_grad: bfloat16 [98304, 128], P(('blk', 'rep'))
The draws below stay inside these ranges and needn't reach their ends.
Inputs may be any that keep to these rules, and one draw needn't show every extreme that they name: `tile_count`: on every device the live slots (count above 0) come first and the rest hold 0; between a quarter and all of a device's 96 slots are live, all of them on at least one device; slot 0 of every device holds 16384. A tile's live entries are its first count entries in row-major order; the others are ignored.
All inputs are finite; a program needn't handle non-finite values.
Results may differ from the reference program's by a relative error of at most 0.015.
Values may be sent and summed in bfloat16 or wider, within the bound.
No kernel may reach another device: no remote copies, remote signals or barrier semaphores. Data moves between devices by JAX's collectives and lax.ppermute only.
A program may use at most 32 MiB of HBM per device.

```python
from functools import partial
import jax
import jax.numpy as jnp
from jax import lax

F = 128
H = 256
TILE = 128
RB_DEV = 1
TILES_DEV = 96
ROWS = 128
TEAMS = 32
MEMBERS = 24
NODES = 98304


def draw_tile_count(key, part):
    key = jax.random.fold_in(key, 7)
    key_live = jax.random.fold_in(key, 1)
    key_count = jax.random.fold_in(key, 2)
    live_slots = jax.random.randint(key_live, (TEAMS, MEMBERS, 1), TILES_DEV // 4, TILES_DEV + 1)
    first_device = lax.broadcasted_iota(jnp.int32, (TEAMS, MEMBERS, 1), 0) + lax.broadcasted_iota(jnp.int32, (TEAMS, MEMBERS, 1), 1) == 0
    live_slots = jnp.where(first_device, TILES_DEV, live_slots)
    counts = jax.random.randint(key_count, (TEAMS, MEMBERS, TILES_DEV), 1, TILE * TILE + 1)
    slot_index = lax.broadcasted_iota(jnp.int32, (TEAMS, MEMBERS, TILES_DEV), 2)
    counts = jnp.where(slot_index == 0, TILE * TILE, counts)
    return jnp.where(slot_index < live_slots, counts, 0).astype(jnp.int32)


def with_ends(array, own_key, least, high):
    dims = array.shape
    spot = [jax.random.randint(jax.random.fold_in(own_key, axis), (), 0, dims[axis]) for axis in range(len(dims))]
    array = array.at[tuple(spot)].set(least)
    longest = dims.index(max(dims))
    spot[longest] = (spot[longest] + 1) % dims[longest]
    return array.at[tuple(spot)].set(high)


def block_scale(key, dims, cuts, least, largest):
    factor_of = 1.0
    for axis_at, shards_of in cuts:
        draws = jax.random.uniform(jax.random.fold_in(jax.random.fold_in(key, 6), axis_at), (shards_of,), jnp.float32, least / len(cuts), largest / len(cuts))
        factor_of = factor_of * jnp.repeat(jnp.exp(draws), dims[axis_at] // shards_of).reshape((-1,) + (1,) * (len(dims) - 1 - axis_at))
    return factor_of


def scatter_about(stream_key, dims, width, reach, shards=(), kind=jnp.bfloat16):
    result = jax.random.normal(stream_key, dims, jnp.float32) * width
    if len(shards) > 0:
        result = block_scale(stream_key, dims, shards, -0.22, 0.18) * result
    return jnp.clip(result, min=-reach, max=reach).astype(kind)


def setup_inputs(seed: int = 0) -> dict:
    key_list = jax.random.split(jax.random.key(seed), 9)
    return {
        "features": scatter_about(key_list[0], (NODES, F), 1.0, 6.0, ((0, 768),)),
        "w_self": scatter_about(key_list[1], (F, H), F ** -0.5, 0.5),
        "w_neigh": scatter_about(key_list[2], (F, H), F ** -0.5, 0.5),
        "cotangent": scatter_about(key_list[3], (NODES, H), 1.0, 6.0, ((0, 768),)),
        "tile_values": scatter_about(key_list[4], (TEAMS, MEMBERS, TILES_DEV, TILE, TILE), (TILE * TILES_DEV // RB_DEV) ** -0.5, 0.0546875, ((0, 32), (1, 24))),
        "tile_row": with_ends(jax.random.randint(key_list[5], (TEAMS, MEMBERS, TILES_DEV), 0, TEAMS * RB_DEV), jax.random.fold_in(key_list[5], 1), 0, (TEAMS * RB_DEV) - 1).astype(jnp.int32),
        "tile_col": with_ends(jax.random.randint(key_list[6], (TEAMS, MEMBERS, TILES_DEV), 0, MEMBERS * RB_DEV), jax.random.fold_in(key_list[6], 1), 0, (MEMBERS * RB_DEV) - 1).astype(jnp.int32),
        "tile_count": draw_tile_count(jax.random.fold_in(key_list[8], 71), 0),
    }


def silu_parts(preact):
    sigmoid_pre = jax.nn.sigmoid(preact)
    return preact * sigmoid_pre, sigmoid_pre * (1.0 + preact * (1.0 - sigmoid_pre))


def masked_tiles(tile_values, tile_count):
    tile_side = tile_values.shape[-1]
    positions = lax.broadcasted_iota(jnp.int32, (tile_side, tile_side), 0) * tile_side + lax.broadcasted_iota(jnp.int32, (tile_side, tile_side), 1)
    return jnp.where(positions < tile_count[..., None, None], tile_values, jnp.zeros_like(tile_values))


def pick_blocks(source, indices):
    return source[indices]


def reference(features, w_self, w_neigh, cotangent, tile_values, tile_row, tile_col, tile_count):
    team_features = features.reshape(TEAMS, MEMBERS * RB_DEV, TILE, F)

    def forward_step(running, inputs):
        block_feats, values, row_ids, col_ids, counts = inputs
        masked = masked_tiles(values, counts).astype(jnp.float32)
        picked = block_feats[col_ids].astype(jnp.float32)
        products = jnp.einsum("mkij,mkjf->mkif", masked, picked)
        summed = jax.vmap(partial(jax.ops.segment_sum, num_segments=TEAMS * RB_DEV))(products, row_ids)
        summed = summed.reshape(MEMBERS, TEAMS, ROWS, F).transpose(1, 0, 2, 3)
        return running + summed, None

    running_start = jnp.zeros((TEAMS, MEMBERS, ROWS, F), jnp.float32)
    totals, _ = lax.scan(forward_step, running_start, (team_features, tile_values, tile_row, tile_col, tile_count))
    aggregate = totals.reshape(NODES, F).astype(jnp.bfloat16)
    preact = jnp.dot(features, w_self, preferred_element_type=jnp.float32) + jnp.dot(aggregate, w_neigh, preferred_element_type=jnp.float32)
    activated_full, derivative = silu_parts(preact)
    activated = activated_full.astype(jnp.bfloat16)
    pre_grad = (cotangent.astype(jnp.float32) * derivative).astype(jnp.bfloat16)
    neighbor_grad = jnp.dot(pre_grad, w_neigh.T, preferred_element_type=jnp.float32).astype(jnp.bfloat16)
    self_part = jnp.dot(pre_grad, w_self.T, preferred_element_type=jnp.float32)
    member_grads = neighbor_grad.reshape(TEAMS, MEMBERS, RB_DEV, TILE, F).transpose(1, 0, 2, 3, 4).reshape(MEMBERS, TEAMS * RB_DEV, TILE, F)

    def backward_step(carry, inputs):
        values, row_ids, col_ids, counts = inputs
        masked = masked_tiles(values, counts).astype(jnp.float32)
        chosen = jax.vmap(pick_blocks)(member_grads, row_ids).astype(jnp.float32)
        products = jnp.einsum("mkij,mkif->mkjf", masked, chosen)
        summed = jax.vmap(partial(jax.ops.segment_sum, num_segments=MEMBERS * RB_DEV))(products, col_ids)
        return carry, jnp.sum(summed, axis=0).reshape(MEMBERS * ROWS, F)

    _, team_grads = lax.scan(backward_step, jnp.zeros((), jnp.float32), (tile_values, tile_row, tile_col, tile_count))
    input_grad = (self_part + team_grads.reshape(NODES, F)).astype(jnp.bfloat16)
    return activated, input_grad
```

```python
import jax
import jax.numpy as jnp
from jax import lax
from jax.experimental import pallas as pl
from jax.experimental.pallas import tpu as pltpu
from jax.sharding import PartitionSpec as P

UNROLL = 8
CORES = 2
VMEM_BYTES = 40 * 1024 * 1024
SMEM_SPEC = pl.BlockSpec(memory_space=pltpu.SMEM)
VMEM_SPEC = pl.BlockSpec(memory_space=pltpu.VMEM)


def kernel_params():
    return pltpu.CompilerParams(vmem_limit_bytes=VMEM_BYTES)


def tile_positions(side):
    return lax.broadcasted_iota(jnp.int32, (side, side), 0) * side + lax.broadcasted_iota(
        jnp.int32, (side, side), 1
    )


def live_part(tile_ref, count_ref, k, positions):
    tile = tile_ref[k]
    return jnp.where(positions < count_ref[k], tile, jnp.zeros_like(tile))


def block_slot(row, core, chips):
    return ((row % CORES) ^ core) * chips + row // CORES


def forward_body(
    core_ref, row_ref, col_ref, count_ref, tile_ref, block_ref, own_ref, other_ref, acc_ref
):
    chips = own_ref.shape[0]
    acc_ref[...] = jnp.zeros_like(acc_ref)
    positions = tile_positions(tile_ref.shape[-1])

    def step(i, carry):
        for u in range(UNROLL):
            k = i * UNROLL + u
            tile = live_part(tile_ref, count_ref, k, positions)
            acc_ref[block_slot(row_ref[k], core_ref[0], chips)] += jnp.dot(
                tile, block_ref[col_ref[k]], preferred_element_type=jnp.float32
            )
        return carry

    lax.fori_loop(0, tile_ref.shape[0] // UNROLL, step, 0)
    own_ref[...] = acc_ref[:chips]
    other_ref[...] = acc_ref[chips:].astype(other_ref.dtype)


def forward(core, ids, tiles, blocks, chips):
    side, width = blocks.shape[1:]
    shape = (chips, side, width)
    return pl.pallas_call(
        forward_body,
        out_shape=(
            jax.ShapeDtypeStruct(shape, jnp.float32),
            jax.ShapeDtypeStruct(shape, jnp.bfloat16),
        ),
        in_specs=[SMEM_SPEC] * 4 + [VMEM_SPEC] * 2,
        out_specs=(VMEM_SPEC, VMEM_SPEC),
        scratch_shapes=[pltpu.VMEM((CORES * chips, side, width), jnp.float32)],
        compiler_params=kernel_params(),
    )(core, *ids, tiles, blocks)


def backward_body(
    core_ref, row_ref, col_ref, count_ref, tile_ref, own_ref, other_ref, out_ref, held_ref, acc_ref
):
    chips = own_ref.shape[0]
    acc_ref[...] = jnp.zeros_like(acc_ref)
    held_ref[:chips] = own_ref[...]
    held_ref[chips:] = other_ref[...]
    positions = tile_positions(tile_ref.shape[-1])

    def step(i, carry):
        for u in range(UNROLL):
            k = i * UNROLL + u
            tile = live_part(tile_ref, count_ref, k, positions)
            acc_ref[col_ref[k]] += jnp.dot(
                held_ref[block_slot(row_ref[k], core_ref[0], chips)],
                tile,
                preferred_element_type=jnp.float32,
            )
        return carry

    lax.fori_loop(0, tile_ref.shape[0] // UNROLL, step, 0)
    out_ref[...] = acc_ref[...].astype(out_ref.dtype)


def backward(core, ids, tiles, own, other, members):
    chips, width, side = own.shape
    return pl.pallas_call(
        backward_body,
        out_shape=jax.ShapeDtypeStruct((members, width, side), jnp.bfloat16),
        in_specs=[SMEM_SPEC] * 4 + [VMEM_SPEC] * 3,
        out_specs=VMEM_SPEC,
        scratch_shapes=[
            pltpu.VMEM((CORES * chips, width, side), jnp.bfloat16),
            pltpu.VMEM((members, width, side), jnp.float32),
        ],
        compiler_params=kernel_params(),
    )(core, *ids, tiles, own, other)


def dense_body(
    feature_ref, part_ref, cotangent_ref, self_ref, neigh_ref, activated_ref, copies_ref, own_ref
):
    aggregate = part_ref[0].astype(jnp.float32)
    for i in range(1, part_ref.shape[0]):
        aggregate += part_ref[i].astype(jnp.float32)
    preact = jnp.dot(
        feature_ref[...], self_ref[...], preferred_element_type=jnp.float32
    ) + jnp.dot(
        aggregate.astype(jnp.bfloat16), neigh_ref[...], preferred_element_type=jnp.float32
    )
    sigmoid_pre = 1.0 / (1.0 + jnp.exp(-preact))
    activated_ref[...] = (preact * sigmoid_pre).astype(jnp.bfloat16)
    derivative = sigmoid_pre * (1.0 + preact * (1.0 - sigmoid_pre))
    pre_grad = (cotangent_ref[...].astype(jnp.float32) * derivative).astype(jnp.bfloat16)
    across = (((1,), (1,)), ((), ()))
    neighbor = lax.dot_general(
        neigh_ref[...], pre_grad, across, preferred_element_type=jnp.float32
    ).astype(jnp.bfloat16)
    for i in range(copies_ref.shape[0]):
        copies_ref[i] = neighbor
    own_ref[...] = lax.dot_general(
        self_ref[...], pre_grad, across, preferred_element_type=jnp.float32
    )


def dense(features, parts, cotangent, w_self, w_neigh):
    rows, width = features.shape
    return pl.pallas_call(
        dense_body,
        out_shape=(
            jax.ShapeDtypeStruct(cotangent.shape, jnp.bfloat16),
            jax.ShapeDtypeStruct((parts.shape[0], width, rows), jnp.bfloat16),
            jax.ShapeDtypeStruct((width, rows), jnp.float32),
        ),
        compiler_params=kernel_params(),
    )(features, parts, cotangent, w_self, w_neigh)


def finish_body(own_ref, part_ref, out_ref):
    total = own_ref[...]
    for i in range(part_ref.shape[0]):
        total += part_ref[i].astype(jnp.float32)
    out_ref[...] = total.T.astype(jnp.bfloat16)


def finish(own, parts):
    width, rows = own.shape
    return pl.pallas_call(
        finish_body,
        out_shape=jax.ShapeDtypeStruct((rows, width), jnp.bfloat16),
        compiler_params=kernel_params(),
    )(own, parts)


def on_device(features, w_self, w_neigh, cotangent, tile_values, tile_row, tile_col, tile_count):
    teams = lax.axis_size("blk")
    members = lax.axis_size("rep")
    chips = teams // CORES
    same_core = [[chip * CORES + c for chip in range(chips)] for c in range(CORES)]
    to_other_core = [(i, i ^ 1) for i in range(teams)]

    def between_chips(blocks):
        return lax.all_to_all(blocks, "blk", 0, 0, axis_index_groups=same_core, tiled=True)

    def between_members(blocks):
        return lax.all_to_all(blocks, "rep", 0, 0, tiled=True)

    core = (lax.axis_index("blk") % CORES).astype(jnp.int32).reshape(1)
    tiles = tile_values[0, 0]
    ids = (tile_row[0, 0], tile_col[0, 0], tile_count[0, 0])
    team_rows = between_members(jnp.broadcast_to(features[None], (members,) + features.shape))
    own_sums, other_sums = forward(core, ids, tiles, team_rows, chips)
    met = lax.ppermute(other_sums, "blk", to_other_core)
    chip_sums = (own_sums + met.astype(jnp.float32)).astype(jnp.bfloat16)
    activated, copies, own_grad = dense(
        features, between_chips(chip_sums), cotangent, w_self, w_neigh
    )
    own_held = between_chips(copies)
    other_held = lax.ppermute(own_held, "blk", to_other_core)
    column_terms = backward(core, ids, tiles, own_held, other_held, members)
    input_grad = finish(own_grad, between_members(column_terms))
    return activated, input_grad


def solution(mesh):
    placed = (
        P(("blk", "rep"), None),
        P(),
        P(),
        P(("blk", "rep"), None),
        P("blk", "rep", None, None, None),
        P("blk", "rep", None),
        P("blk", "rep", None),
        P("blk", "rep", None),
    )
    return jax.shard_map(
        on_device,
        mesh=mesh,
        in_specs=placed,
        out_specs=(P(("blk", "rep"), None), P(("blk", "rep"), None)),
        check_vma=False,
    )
```

```python
import jax
import jax.numpy as jnp
from jax import lax
from jax.experimental import pallas as pl
from jax.experimental.pallas import tpu as pltpu
from jax.sharding import PartitionSpec as P

UNROLL = 8
CORES = 2
LANES = 2
VMEM_BYTES = 40 * 1024 * 1024
SMEM_SPEC = pl.BlockSpec(memory_space=pltpu.SMEM)
VMEM_SPEC = pl.BlockSpec(memory_space=pltpu.VMEM)


def kernel_params():
    return pltpu.CompilerParams(vmem_limit_bytes=VMEM_BYTES)


def tile_positions(side):
    return lax.broadcasted_iota(jnp.int32, (side, side), 0) * side + lax.broadcasted_iota(
        jnp.int32, (side, side), 1
    )


def mask_body(count_ref, tile_ref, out_ref):
    positions = tile_positions(tile_ref.shape[-1])

    def step(i, carry):
        for u in range(UNROLL):
            k = i * UNROLL + u
            tile = tile_ref[k]
            out_ref[k] = jnp.where(positions < count_ref[k], tile, jnp.zeros_like(tile))
        return carry

    lax.fori_loop(0, tile_ref.shape[0] // UNROLL, step, 0)


def live_tiles(counts, tiles):
    return pl.pallas_call(
        mask_body,
        out_shape=jax.ShapeDtypeStruct(tiles.shape, tiles.dtype),
        in_specs=[SMEM_SPEC, VMEM_SPEC],
        out_specs=VMEM_SPEC,
        compiler_params=kernel_params(),
        cost_estimate=pl.CostEstimate(
            flops=tiles.size, bytes_accessed=4 * tiles.size, transcendentals=0
        ),
    )(counts, tiles)


def forward_body(
    id_ref, tile_ref, near_ref, far_ref, own_ref, other_ref, held_ref, acc_ref
):
    depth = near_ref.shape[0]
    half = own_ref.shape[0]
    acc_ref[...] = jnp.zeros_like(acc_ref)
    held_ref[:depth] = near_ref[...]
    held_ref[depth:] = far_ref[...]

    def step(i, carry):
        for u in range(UNROLL):
            k = i * UNROLL + u
            acc_ref[id_ref[0, k]] += jnp.dot(
                tile_ref[k], held_ref[id_ref[1, k]], preferred_element_type=jnp.float32
            )
        return carry

    lax.fori_loop(0, tile_ref.shape[0] // UNROLL, step, 0)
    own_ref[...] = acc_ref[:half]
    other_ref[...] = acc_ref[half:].astype(other_ref.dtype)


def forward(ids, tiles, near, far, half):
    depth, side, width = near.shape
    shape = (half, side, width)
    return pl.pallas_call(
        forward_body,
        out_shape=(
            jax.ShapeDtypeStruct(shape, jnp.float32),
            jax.ShapeDtypeStruct(shape, jnp.bfloat16),
        ),
        in_specs=[SMEM_SPEC] + [VMEM_SPEC] * 3,
        out_specs=(VMEM_SPEC, VMEM_SPEC),
        scratch_shapes=[
            pltpu.VMEM((2 * depth, side, width), jnp.bfloat16),
            pltpu.VMEM((2 * half, side, width), jnp.float32),
        ],
        compiler_params=kernel_params(),
    )(ids, tiles, near, far)


def backward_body(
    id_ref, tile_ref, near_ref, far_ref, own_ref, other_ref, held_ref, acc_ref
):
    chips = near_ref.shape[0]
    half = own_ref.shape[0]
    acc_ref[...] = jnp.zeros_like(acc_ref)
    held_ref[:chips] = near_ref[...]
    held_ref[chips:] = far_ref[...]

    def step(i, carry):
        for u in range(UNROLL):
            k = i * UNROLL + u
            acc_ref[id_ref[1, k]] += jnp.dot(
                held_ref[id_ref[0, k]], tile_ref[k], preferred_element_type=jnp.float32
            )
        return carry

    lax.fori_loop(0, tile_ref.shape[0] // UNROLL, step, 0)
    own_ref[...] = acc_ref[:half]
    other_ref[...] = acc_ref[half:].astype(other_ref.dtype)


def backward(ids, tiles, near, far, half):
    chips, width, side = near.shape
    shape = (half, width, side)
    return pl.pallas_call(
        backward_body,
        out_shape=(
            jax.ShapeDtypeStruct(shape, jnp.float32),
            jax.ShapeDtypeStruct(shape, jnp.bfloat16),
        ),
        in_specs=[SMEM_SPEC] + [VMEM_SPEC] * 3,
        out_specs=(VMEM_SPEC, VMEM_SPEC),
        scratch_shapes=[
            pltpu.VMEM((2 * chips, width, side), jnp.bfloat16),
            pltpu.VMEM((2 * half, width, side), jnp.float32),
        ],
        compiler_params=kernel_params(),
    )(ids, tiles, near, far)


def dense_body(
    feature_ref, part_ref, cotangent_ref, self_ref, neigh_ref, activated_ref, copies_ref, own_ref
):
    aggregate = part_ref[0].astype(jnp.float32)
    for i in range(1, part_ref.shape[0]):
        aggregate += part_ref[i].astype(jnp.float32)
    preact = jnp.dot(
        feature_ref[...], self_ref[...], preferred_element_type=jnp.float32
    ) + jnp.dot(
        aggregate.astype(jnp.bfloat16), neigh_ref[...], preferred_element_type=jnp.float32
    )
    sigmoid_pre = 1.0 / (1.0 + jnp.exp(-preact))
    activated_ref[...] = (preact * sigmoid_pre).astype(jnp.bfloat16)
    derivative = sigmoid_pre * (1.0 + preact * (1.0 - sigmoid_pre))
    pre_grad = (cotangent_ref[...].astype(jnp.float32) * derivative).astype(jnp.bfloat16)
    across = (((1,), (1,)), ((), ()))
    neighbor = lax.dot_general(
        neigh_ref[...], pre_grad, across, preferred_element_type=jnp.float32
    ).astype(jnp.bfloat16)
    for i in range(copies_ref.shape[0]):
        copies_ref[i] = neighbor
    own_ref[...] = lax.dot_general(
        self_ref[...], pre_grad, across, preferred_element_type=jnp.float32
    )


def dense(features, parts, cotangent, w_self, w_neigh):
    rows, width = features.shape
    return pl.pallas_call(
        dense_body,
        out_shape=(
            jax.ShapeDtypeStruct(cotangent.shape, jnp.bfloat16),
            jax.ShapeDtypeStruct((parts.shape[0], width, rows), jnp.bfloat16),
            jax.ShapeDtypeStruct((width, rows), jnp.float32),
        ),
        compiler_params=kernel_params(),
    )(features, parts, cotangent, w_self, w_neigh)


def finish_body(own_ref, part_ref, out_ref):
    total = own_ref[...]
    for i in range(part_ref.shape[0]):
        total += part_ref[i].astype(jnp.float32)
    out_ref[...] = total.T.astype(jnp.bfloat16)


def finish(own, parts):
    width, rows = own.shape
    return pl.pallas_call(
        finish_body,
        out_shape=jax.ShapeDtypeStruct((rows, width), jnp.bfloat16),
        compiler_params=kernel_params(),
    )(own, parts)


def on_device(features, w_self, w_neigh, cotangent, tile_values, tile_row, tile_col, tile_count):
    teams = lax.axis_size("blk")
    members = lax.axis_size("rep")
    chips = teams // CORES
    depth = members // LANES
    same_core = [[chip * CORES + c for chip in range(chips)] for c in range(CORES)]
    same_lane = [[lane * depth + z for z in range(depth)] for lane in range(LANES)]
    to_other_core = [(i, i ^ 1) for i in range(teams)]
    to_other_lane = [(i, (i + depth) % members) for i in range(members)]

    def between_chips(blocks):
        return lax.all_to_all(blocks, "blk", 0, 0, axis_index_groups=same_core, tiled=True)

    def along_depth(blocks):
        return lax.all_to_all(blocks, "rep", 0, 0, axis_index_groups=same_lane, tiled=True)

    core = (lax.axis_index("blk") % CORES).astype(jnp.int32)
    lane = (lax.axis_index("rep") // depth).astype(jnp.int32)
    row, col = tile_row[0, 0], tile_col[0, 0]
    ids = jnp.stack(
        [
            ((row % CORES) ^ core) * chips + row // CORES,
            ((col // depth) ^ lane) * depth + col % depth,
        ]
    )
    tiles = live_tiles(tile_count[0, 0], tile_values[0, 0])
    lane_rows = along_depth(jnp.broadcast_to(features[None], (depth,) + features.shape))
    lane_rows, tiles, ids = lax.optimization_barrier((lane_rows, tiles, ids))
    far_rows = lax.ppermute(lane_rows, "rep", to_other_lane)
    own_sums, other_sums = forward(ids, tiles, lane_rows, far_rows, chips)
    met = lax.ppermute(other_sums, "blk", to_other_core)
    chip_sums = (own_sums + met.astype(jnp.float32)).astype(jnp.bfloat16)
    activated, copies, own_grad = dense(
        features, between_chips(chip_sums), cotangent, w_self, w_neigh
    )
    near = between_chips(copies)
    far = lax.ppermute(near, "blk", to_other_core)
    own_terms, other_terms = backward(ids, tiles, near, far, depth)
    met = lax.ppermute(other_terms, "rep", to_other_lane)
    lane_terms = (own_terms + met.astype(jnp.float32)).astype(jnp.bfloat16)
    input_grad = finish(own_grad, along_depth(lane_terms))
    return activated, input_grad


def solution(mesh):
    placed = (
        P(("blk", "rep"), None),
        P(),
        P(),
        P(("blk", "rep"), None),
        P("blk", "rep", None, None, None),
        P("blk", "rep", None),
        P("blk", "rep", None),
        P("blk", "rep", None),
    )
    return jax.shard_map(
        on_device,
        mesh=mesh,
        in_specs=placed,
        out_specs=(P(("blk", "rep"), None), P(("blk", "rep"), None)),
        check_vma=False,
    )
```

```python
import functools

import jax
import jax.numpy as jnp
from jax import lax
from jax.experimental import pallas as pl
from jax.experimental.pallas import tpu as pltpu
from jax.sharding import PartitionSpec as P

STEP = 12
CORES = 2
LANES = 2
FIELD = 5
VMEM_BYTES = 32 * 1024 * 1024
SMEM_SPEC = pl.BlockSpec(memory_space=pltpu.SMEM)
VMEM_SPEC = pl.BlockSpec(memory_space=pltpu.VMEM)

OWN_OWN, OTHER_OWN, OTHER_OTHER, OWN_OTHER = range(4)
CLASSES = 4


def kernel_params():
    return pltpu.CompilerParams(vmem_limit_bytes=VMEM_BYTES)


def copies_body(block_ref, out_ref):
    block = block_ref[...]
    for i in range(out_ref.shape[0]):
        out_ref[i] = block


def copies_of(block, count):
    return pl.pallas_call(
        copies_body,
        out_shape=jax.ShapeDtypeStruct((count,) + block.shape, block.dtype),
        in_specs=[VMEM_SPEC],
        out_specs=VMEM_SPEC,
        compiler_params=kernel_params(),
    )(block)


def plan_body(chips, depth, here_ref, row_ref, col_ref, count_ref, tile_ref, order_ref, bound_ref, out_ref):
    slots, side, _ = tile_ref.shape
    positions = lax.broadcasted_iota(jnp.int32, (side, side), 0) * side + lax.broadcasted_iota(
        jnp.int32, (side, side), 1
    )

    def mask(i, carry):
        for u in range(8):
            k = i * 8 + u
            tile = tile_ref[k]
            out_ref[k] = jnp.where(positions < count_ref[k], tile, jnp.zeros_like(tile))
        return carry

    lax.fori_loop(0, slots // 8, mask, 0)
    out_ref[slots] = jnp.zeros((side, side), out_ref.dtype)

    def place(k):
        row, col = row_ref[k], col_ref[k]
        other_row = lax.rem(row, CORES) ^ here_ref[0]
        other_col = lax.div(col, depth) ^ here_ref[1]
        kind = 2 * other_col + (other_col ^ other_row)
        chip = lax.div(row, CORES)
        lane = lax.div(col, depth)
        level = lax.rem(col, depth)
        turned = (lane * 2 + lax.rem(level, 2)) * (depth // 2) + lax.div(level, 2)
        return kind, k + ((chip + ((col + (turned << FIELD)) << FIELD)) << 8)

    def tally(k, counts):
        kind, _ = place(k)
        return tuple(n + (kind == c).astype(jnp.int32) for c, n in enumerate(counts))

    zero = jnp.int32(0)
    counts = lax.fori_loop(0, slots, tally, (zero,) * CLASSES)
    starts = [zero]
    for n in counts:
        starts.append(starts[-1] + n)
    for c, start in enumerate(starts):
        bound_ref[c] = start

    def put(k, nexts):
        kind, code = place(k)
        spot = nexts[0]
        for c in range(1, CLASSES):
            spot = jnp.where(kind == c, nexts[c], spot)
        order_ref[spot] = code
        return tuple(n + (kind == c).astype(jnp.int32) for c, n in enumerate(nexts))

    lax.fori_loop(0, slots, put, tuple(starts[:CLASSES]))


def plan(here, rows, cols, counts, tiles, chips, depth):
    slots, side, _ = tiles.shape
    return pl.pallas_call(
        functools.partial(plan_body, chips, depth),
        out_shape=(
            jax.ShapeDtypeStruct((slots,), jnp.int32),
            jax.ShapeDtypeStruct((CLASSES + 1,), jnp.int32),
            jax.ShapeDtypeStruct((slots + 1, side, side), tiles.dtype),
        ),
        in_specs=[SMEM_SPEC] * 4 + [VMEM_SPEC],
        out_specs=(SMEM_SPEC, SMEM_SPEC, VMEM_SPEC),
        compiler_params=kernel_params(),
        cost_estimate=pl.CostEstimate(
            flops=tiles.size, bytes_accessed=4 * tiles.size, transcendentals=0
        ),
    )(here, rows, cols, counts, tiles)


def add_products(kind, forward, order_ref, bound_ref, tile_ref, block_ref, sum_ref):
    start, end = bound_ref[kind], bound_ref[kind + 1]
    slots = order_ref.shape[0]
    empty = tile_ref.shape[0] - 1

    def step(i, carry):
        for u in range(STEP):
            at = start + i * STEP + u
            code = jnp.where(at < end, order_ref[jnp.minimum(at, slots - 1)], empty)
            tile = tile_ref[code & 255]
            chip = (code >> 8) & ((1 << FIELD) - 1)
            if forward:
                level = (code >> (8 + FIELD)) & ((1 << FIELD) - 1)
                sum_ref[chip] += jnp.dot(
                    tile, block_ref[level], preferred_element_type=jnp.float32
                )
            else:
                turned = code >> (8 + 2 * FIELD)
                sum_ref[turned] += jnp.dot(
                    block_ref[chip], tile, preferred_element_type=jnp.float32
                )
        return carry

    lax.fori_loop(0, lax.div(end - start + (STEP - 1), STEP), step, 0)


def leaving_body(order_ref, bound_ref, tile_ref, block_ref, out_ref, total_ref):
    total_ref[...] = jnp.zeros_like(total_ref)
    for kind in (OTHER_OWN, OTHER_OTHER):
        add_products(kind, True, order_ref, bound_ref, tile_ref, block_ref, total_ref)
    out_ref[...] = total_ref[...].astype(out_ref.dtype)


def staying_body(order_ref, bound_ref, tile_ref, block_ref, total_ref):
    total_ref[...] = jnp.zeros_like(total_ref)
    for kind in (OWN_OWN, OWN_OTHER):
        add_products(kind, True, order_ref, bound_ref, tile_ref, block_ref, total_ref)


def own_rows_body(order_ref, bound_ref, tile_ref, block_ref, sum_ref):
    sum_ref[...] = jnp.zeros_like(sum_ref)
    for kind in (OWN_OWN, OWN_OTHER):
        add_products(kind, False, order_ref, bound_ref, tile_ref, block_ref, sum_ref)


def other_rows_body(order_ref, bound_ref, tile_ref, block_ref, sum_ref, out_ref, total_ref):
    total_ref[...] = sum_ref[...]
    for kind in (OTHER_OWN, OTHER_OTHER):
        add_products(kind, False, order_ref, bound_ref, tile_ref, block_ref, total_ref)
    out_ref[...] = total_ref[...].astype(out_ref.dtype)


def tile_products(body, tiles, blocks, sums, out_shapes, scratch, cost):
    order, bound, values = tiles
    operands = (order, bound, values, blocks) + sums
    return pl.pallas_call(
        body,
        out_shape=out_shapes,
        in_specs=[SMEM_SPEC] * 2 + [VMEM_SPEC] * (len(operands) - 2),
        out_specs=(VMEM_SPEC,) * len(out_shapes),
        scratch_shapes=scratch,
        compiler_params=kernel_params(),
        cost_estimate=pl.CostEstimate(flops=cost, bytes_accessed=cost // 128, transcendentals=0),
    )(*operands)


def stack_of(count, side, width, kind):
    return jax.ShapeDtypeStruct((count, side, width), kind)


def forward_sums(tiles, blocks, swap, chips):
    side, width = blocks.shape[1:]
    full = stack_of(chips, side, width, jnp.float32)
    half = stack_of(chips, side, width, jnp.bfloat16)
    cost = tiles[2].size * width
    total = (pltpu.VMEM(full.shape, jnp.float32),)
    (leaving,) = tile_products(leaving_body, tiles, blocks, (), (half,), total, cost)
    met = swap(leaving)
    (own,) = tile_products(staying_body, tiles, blocks, (), (full,), (), cost)
    return (own + met.astype(jnp.float32)).astype(jnp.bfloat16)


def backward_sums(tiles, near, send, square, members):
    width, side = near.shape[1:]
    full = stack_of(members, width, side, jnp.float32)
    half = stack_of(members, width, side, jnp.bfloat16)
    cost = tiles[2].size * width
    far = send(near)
    (own,) = tile_products(own_rows_body, tiles, near, (), (full,), (), cost)
    total = (pltpu.VMEM(full.shape, jnp.float32),)
    (sums,) = tile_products(other_rows_body, tiles, far, (own,), (half,), total, cost)
    met = square(sums).reshape(2 * LANES, -1, width, side).astype(jnp.float32)
    return (met[0] + met[1] + met[2] + met[3]).astype(jnp.bfloat16)


def dense_body(
    feature_ref, part_ref, cotangent_ref, self_ref, neigh_ref, activated_ref, copies_ref, own_ref
):
    aggregate = part_ref[0].astype(jnp.float32)
    for i in range(1, part_ref.shape[0]):
        aggregate += part_ref[i].astype(jnp.float32)
    preact = jnp.dot(
        feature_ref[...], self_ref[...], preferred_element_type=jnp.float32
    ) + jnp.dot(
        aggregate.astype(jnp.bfloat16), neigh_ref[...], preferred_element_type=jnp.float32
    )
    sigmoid_pre = 1.0 / (1.0 + jnp.exp(-preact))
    activated_ref[...] = (preact * sigmoid_pre).astype(jnp.bfloat16)
    derivative = sigmoid_pre * (1.0 + preact * (1.0 - sigmoid_pre))
    pre_grad = (cotangent_ref[...].astype(jnp.float32) * derivative).astype(jnp.bfloat16)
    across = (((1,), (1,)), ((), ()))
    neighbor = lax.dot_general(
        neigh_ref[...], pre_grad, across, preferred_element_type=jnp.float32
    ).astype(jnp.bfloat16)
    for i in range(copies_ref.shape[0]):
        copies_ref[i] = neighbor
    own_ref[...] = lax.dot_general(
        self_ref[...], pre_grad, across, preferred_element_type=jnp.float32
    )


def dense(features, parts, cotangent, w_self, w_neigh):
    rows, width = features.shape
    return pl.pallas_call(
        dense_body,
        out_shape=(
            jax.ShapeDtypeStruct(cotangent.shape, jnp.bfloat16),
            jax.ShapeDtypeStruct((parts.shape[0], width, rows), jnp.bfloat16),
            jax.ShapeDtypeStruct((width, rows), jnp.float32),
        ),
        compiler_params=kernel_params(),
    )(features, parts, cotangent, w_self, w_neigh)


def finish_body(own_ref, part_ref, out_ref):
    total = own_ref[...]
    for i in range(part_ref.shape[0]):
        total += part_ref[i].astype(jnp.float32)
    out_ref[...] = total.T.astype(jnp.bfloat16)


def finish(own, parts):
    width, rows = own.shape
    return pl.pallas_call(
        finish_body,
        out_shape=jax.ShapeDtypeStruct((rows, width), jnp.bfloat16),
        compiler_params=kernel_params(),
    )(own, parts)


def on_device(features, w_self, w_neigh, cotangent, tile_values, tile_row, tile_col, tile_count):
    teams = lax.axis_size("blk")
    members = lax.axis_size("rep")
    chips = teams // CORES
    depth = members // LANES
    same_core = [[chip * CORES + c for chip in range(chips)] for c in range(CORES)]
    same_lane = [[lane * depth + z for z in range(depth)] for lane in range(LANES)]
    same_parity = [
        [lane * depth + z for z in range(parity, depth, 2)]
        for lane in range(LANES)
        for parity in range(2)
    ]
    squares = [
        [lane * depth + z + parity for lane in range(LANES) for parity in range(2)]
        for z in range(0, depth, 2)
    ]
    to_other_core = [(i, i ^ 1) for i in range(teams)]
    same_level = [[lane * depth + z for lane in range(LANES)] for z in range(depth)]

    def between_chips(blocks):
        return lax.all_to_all(blocks, "blk", 0, 0, axis_index_groups=same_core, tiled=True)

    def along_depth(blocks):
        return lax.all_to_all(blocks, "rep", 0, 0, axis_index_groups=same_lane, tiled=True)

    def swap_cores(blocks):
        return lax.ppermute(blocks, "blk", to_other_core)

    def in_square(blocks):
        return lax.all_to_all(blocks, "rep", 0, 0, axis_index_groups=squares, tiled=True)

    def along_parity(blocks):
        return lax.all_to_all(blocks, "rep", 0, 0, axis_index_groups=same_parity, tiled=True)

    member = lax.axis_index("rep")
    here = jnp.stack([lax.axis_index("blk") % CORES, member // depth]).astype(jnp.int32)
    tiles = plan(
        here, tile_row[0, 0], tile_col[0, 0], tile_count[0, 0], tile_values[0, 0], chips, depth
    )
    lane_rows = along_depth(copies_of(features, depth))
    lane_rows, tiles = lax.optimization_barrier((lane_rows, tiles))
    team_rows = lax.all_gather(
        lane_rows, "rep", axis=0, tiled=True, axis_index_groups=same_level
    )
    chip_sums = forward_sums(tiles, team_rows, swap_cores, chips)
    activated, copies, own_grad = dense(
        features, between_chips(chip_sums), cotangent, w_self, w_neigh
    )
    held = between_chips(copies)
    lane_terms = backward_sums(tiles, held, swap_cores, in_square, members)
    input_grad = finish(own_grad, along_parity(lane_terms))
    return activated, input_grad


def solution(mesh):
    placed = (
        P(("blk", "rep"), None),
        P(),
        P(),
        P(("blk", "rep"), None),
        P("blk", "rep", None, None, None),
        P("blk", "rep", None),
        P("blk", "rep", None),
        P("blk", "rep", None),
    )
    return jax.shard_map(
        on_device,
        mesh=mesh,
        in_specs=placed,
        out_specs=(P(("blk", "rep"), None), P(("blk", "rep"), None)),
        check_vma=False,
    )
```

```python
import functools

import jax
import jax.numpy as jnp
from jax import lax
from jax.experimental import pallas as pl
from jax.experimental.pallas import tpu as pltpu
from jax.sharding import PartitionSpec as P

STEP = 32
CORES = 2
LANES = 2
FIELD = 5
VMEM_BYTES = 32 * 1024 * 1024
SMEM_SPEC = pl.BlockSpec(memory_space=pltpu.SMEM)
VMEM_SPEC = pl.BlockSpec(memory_space=pltpu.VMEM)

OWN, OTHER = range(CORES)


def kernel_params():
    return pltpu.CompilerParams(vmem_limit_bytes=VMEM_BYTES)


def copies_body(block_ref, out_ref):
    block = block_ref[...]
    for i in range(out_ref.shape[0]):
        out_ref[i] = block


def copies_of(block, count):
    return pl.pallas_call(
        copies_body,
        out_shape=jax.ShapeDtypeStruct((count,) + block.shape, block.dtype),
        in_specs=[VMEM_SPEC],
        out_specs=VMEM_SPEC,
        compiler_params=kernel_params(),
    )(block)


def plan_body(chips, depth, here_ref, row_ref, col_ref, count_ref, tile_ref, order_ref, bound_ref, out_ref):
    slots, side, _ = tile_ref.shape
    positions = lax.broadcasted_iota(jnp.int32, (side, side), 0) * side + lax.broadcasted_iota(
        jnp.int32, (side, side), 1
    )

    def mask(i, carry):
        for u in range(8):
            k = i * 8 + u
            tile = tile_ref[k]
            out_ref[k] = jnp.where(positions < count_ref[k], tile, jnp.zeros_like(tile))
        return carry

    lax.fori_loop(0, slots // 8, mask, 0)
    out_ref[slots] = jnp.zeros((side, side), out_ref.dtype)

    def place(k):
        row, col = row_ref[k], col_ref[k]
        kind = lax.rem(row, CORES) ^ here_ref[0]
        chip = lax.div(row, CORES)
        lane = lax.div(col, depth)
        level = lax.rem(col, depth)
        turned = (lane * 2 + lax.rem(level, 2)) * (depth // 2) + lax.div(level, 2)
        return kind, k + ((chip + ((col + (turned << FIELD)) << FIELD)) << 8)

    zero = jnp.int32(0)
    others = lax.fori_loop(0, slots, lambda k, n: n + place(k)[0], zero)
    bound_ref[OWN] = zero
    bound_ref[OTHER] = slots - others
    bound_ref[CORES] = jnp.int32(slots)

    def put(k, nexts):
        kind, code = place(k)
        order_ref[jnp.where(kind == OWN, nexts[OWN], nexts[OTHER])] = code
        return nexts[OWN] + (1 - kind), nexts[OTHER] + kind

    lax.fori_loop(0, slots, put, (zero, slots - others))


def plan(here, rows, cols, counts, tiles, chips, depth):
    slots, side, _ = tiles.shape
    return pl.pallas_call(
        functools.partial(plan_body, chips, depth),
        out_shape=(
            jax.ShapeDtypeStruct((slots,), jnp.int32),
            jax.ShapeDtypeStruct((CORES + 1,), jnp.int32),
            jax.ShapeDtypeStruct((slots + 1, side, side), tiles.dtype),
        ),
        in_specs=[SMEM_SPEC] * 4 + [VMEM_SPEC],
        out_specs=(SMEM_SPEC, SMEM_SPEC, VMEM_SPEC),
        compiler_params=kernel_params(),
        cost_estimate=pl.CostEstimate(
            flops=tiles.size, bytes_accessed=4 * tiles.size, transcendentals=0
        ),
    )(here, rows, cols, counts, tiles)


def add_products(kind, forward, order_ref, bound_ref, tile_ref, block_ref, sum_ref):
    start, end = bound_ref[kind], bound_ref[kind + 1]
    slots = order_ref.shape[0]
    empty = tile_ref.shape[0] - 1

    def step(i, carry):
        for u in range(STEP):
            at = start + i * STEP + u
            code = jnp.where(at < end, order_ref[jnp.minimum(at, slots - 1)], empty)
            tile = tile_ref[code & 255]
            chip = (code >> 8) & ((1 << FIELD) - 1)
            if forward:
                level = (code >> (8 + FIELD)) & ((1 << FIELD) - 1)
                sum_ref[chip] += jnp.dot(
                    tile, block_ref[level], preferred_element_type=jnp.float32
                )
            else:
                turned = code >> (8 + 2 * FIELD)
                sum_ref[turned] += jnp.dot(
                    block_ref[chip], tile, preferred_element_type=jnp.float32
                )
        return carry

    lax.fori_loop(0, lax.div(end - start + (STEP - 1), STEP), step, 0)


def leaving_body(order_ref, bound_ref, tile_ref, block_ref, out_ref, total_ref):
    total_ref[...] = jnp.zeros_like(total_ref)
    add_products(OTHER, True, order_ref, bound_ref, tile_ref, block_ref, total_ref)
    out_ref[...] = total_ref[...].astype(out_ref.dtype)


def staying_body(order_ref, bound_ref, tile_ref, block_ref, total_ref):
    total_ref[...] = jnp.zeros_like(total_ref)
    add_products(OWN, True, order_ref, bound_ref, tile_ref, block_ref, total_ref)


def own_rows_body(order_ref, bound_ref, tile_ref, block_ref, sum_ref):
    sum_ref[...] = jnp.zeros_like(sum_ref)
    add_products(OWN, False, order_ref, bound_ref, tile_ref, block_ref, sum_ref)


def other_rows_body(order_ref, bound_ref, tile_ref, block_ref, sum_ref, out_ref, total_ref):
    total_ref[...] = sum_ref[...]
    add_products(OTHER, False, order_ref, bound_ref, tile_ref, block_ref, total_ref)
    out_ref[...] = total_ref[...].astype(out_ref.dtype)


def tile_products(body, tiles, blocks, sums, out_shapes, scratch, cost):
    order, bound, values = tiles
    operands = (order, bound, values, blocks) + sums
    return pl.pallas_call(
        body,
        out_shape=out_shapes,
        in_specs=[SMEM_SPEC] * 2 + [VMEM_SPEC] * (len(operands) - 2),
        out_specs=(VMEM_SPEC,) * len(out_shapes),
        scratch_shapes=scratch,
        compiler_params=kernel_params(),
        cost_estimate=pl.CostEstimate(flops=cost, bytes_accessed=cost // 128, transcendentals=0),
    )(*operands)


def stack_of(count, side, width, kind):
    return jax.ShapeDtypeStruct((count, side, width), kind)


def forward_sums(tiles, blocks, swap, chips):
    side, width = blocks.shape[1:]
    full = stack_of(chips, side, width, jnp.float32)
    half = stack_of(chips, side, width, jnp.bfloat16)
    cost = tiles[2].size * width
    total = (pltpu.VMEM(full.shape, jnp.float32),)
    (leaving,) = tile_products(leaving_body, tiles, blocks, (), (half,), total, cost)
    met = swap(leaving)
    (own,) = tile_products(staying_body, tiles, blocks, (), (full,), (), cost)
    return (own + met.astype(jnp.float32)).astype(jnp.bfloat16)


def backward_sums(tiles, near, send, square, members):
    width, side = near.shape[1:]
    full = stack_of(members, width, side, jnp.float32)
    half = stack_of(members, width, side, jnp.bfloat16)
    cost = tiles[2].size * width
    far = send(near)
    (own,) = tile_products(own_rows_body, tiles, near, (), (full,), (), cost)
    total = (pltpu.VMEM(full.shape, jnp.float32),)
    (sums,) = tile_products(other_rows_body, tiles, far, (own,), (half,), total, cost)
    met = square(sums).reshape(2 * LANES, -1, width, side).astype(jnp.float32)
    return (met[0] + met[1] + met[2] + met[3]).astype(jnp.bfloat16)


def dense_body(
    feature_ref, part_ref, cotangent_ref, self_ref, neigh_ref, activated_ref, copies_ref, own_ref
):
    aggregate = part_ref[0].astype(jnp.float32)
    for i in range(1, part_ref.shape[0]):
        aggregate += part_ref[i].astype(jnp.float32)
    preact = jnp.dot(
        feature_ref[...], self_ref[...], preferred_element_type=jnp.float32
    ) + jnp.dot(
        aggregate.astype(jnp.bfloat16), neigh_ref[...], preferred_element_type=jnp.float32
    )
    sigmoid_pre = 1.0 / (1.0 + jnp.exp(-preact))
    activated_ref[...] = (preact * sigmoid_pre).astype(jnp.bfloat16)
    derivative = sigmoid_pre * (1.0 + preact * (1.0 - sigmoid_pre))
    pre_grad = (cotangent_ref[...].astype(jnp.float32) * derivative).astype(jnp.bfloat16)
    across = (((1,), (1,)), ((), ()))
    neighbor = lax.dot_general(
        neigh_ref[...], pre_grad, across, preferred_element_type=jnp.float32
    ).astype(jnp.bfloat16)
    for i in range(copies_ref.shape[0]):
        copies_ref[i] = neighbor
    own_ref[...] = lax.dot_general(
        self_ref[...], pre_grad, across, preferred_element_type=jnp.float32
    )


def dense(features, parts, cotangent, w_self, w_neigh):
    rows, width = features.shape
    return pl.pallas_call(
        dense_body,
        out_shape=(
            jax.ShapeDtypeStruct(cotangent.shape, jnp.bfloat16),
            jax.ShapeDtypeStruct((parts.shape[0], width, rows), jnp.bfloat16),
            jax.ShapeDtypeStruct((width, rows), jnp.float32),
        ),
        compiler_params=kernel_params(),
    )(features, parts, cotangent, w_self, w_neigh)


def finish_body(own_ref, part_ref, out_ref):
    total = own_ref[...]
    for i in range(part_ref.shape[0]):
        total += part_ref[i].astype(jnp.float32)
    out_ref[...] = total.T.astype(jnp.bfloat16)


def finish(own, parts):
    width, rows = own.shape
    return pl.pallas_call(
        finish_body,
        out_shape=jax.ShapeDtypeStruct((rows, width), jnp.bfloat16),
        compiler_params=kernel_params(),
    )(own, parts)


def on_device(features, w_self, w_neigh, cotangent, tile_values, tile_row, tile_col, tile_count):
    teams = lax.axis_size("blk")
    members = lax.axis_size("rep")
    chips = teams // CORES
    depth = members // LANES
    same_core = [[chip * CORES + c for chip in range(chips)] for c in range(CORES)]
    same_lane = [[lane * depth + z for z in range(depth)] for lane in range(LANES)]
    same_parity = [
        [lane * depth + z for z in range(parity, depth, 2)]
        for lane in range(LANES)
        for parity in range(2)
    ]
    squares = [
        [lane * depth + z + parity for lane in range(LANES) for parity in range(2)]
        for z in range(0, depth, 2)
    ]
    to_other_core = [(i, i ^ 1) for i in range(teams)]
    same_level = [[lane * depth + z for lane in range(LANES)] for z in range(depth)]

    def between_chips(blocks):
        return lax.all_to_all(blocks, "blk", 0, 0, axis_index_groups=same_core, tiled=True)

    def along_depth(blocks):
        return lax.all_to_all(blocks, "rep", 0, 0, axis_index_groups=same_lane, tiled=True)

    def swap_cores(blocks):
        return lax.ppermute(blocks, "blk", to_other_core)

    def in_square(blocks):
        return lax.all_to_all(blocks, "rep", 0, 0, axis_index_groups=squares, tiled=True)

    def along_parity(blocks):
        return lax.all_to_all(blocks, "rep", 0, 0, axis_index_groups=same_parity, tiled=True)

    here = (lax.axis_index("blk") % CORES).astype(jnp.int32).reshape(1)
    tiles = plan(
        here, tile_row[0, 0], tile_col[0, 0], tile_count[0, 0], tile_values[0, 0], chips, depth
    )
    lane_rows = along_depth(copies_of(features, depth))
    lane_rows, tiles = lax.optimization_barrier((lane_rows, tiles))
    team_rows = lax.all_gather(
        lane_rows, "rep", axis=0, tiled=True, axis_index_groups=same_level
    )
    chip_sums = forward_sums(tiles, team_rows, swap_cores, chips)
    activated, copies, own_grad = dense(
        features, between_chips(chip_sums), cotangent, w_self, w_neigh
    )
    held = between_chips(copies)
    lane_terms = backward_sums(tiles, held, swap_cores, in_square, members)
    input_grad = finish(own_grad, along_parity(lane_terms))
    return activated, input_grad


def solution(mesh):
    placed = (
        P(("blk", "rep"), None),
        P(),
        P(),
        P(("blk", "rep"), None),
        P("blk", "rep", None, None, None),
        P("blk", "rep", None),
        P("blk", "rep", None),
        P("blk", "rep", None),
    )
    return jax.shard_map(
        on_device,
        mesh=mesh,
        in_specs=placed,
        out_specs=(P(("blk", "rep"), None), P(("blk", "rep"), None)),
        check_vma=False,
    )
```

```python
import functools

import jax
import jax.numpy as jnp
from jax import lax
from jax.experimental import pallas as pl
from jax.experimental.pallas import tpu as pltpu
from jax.sharding import PartitionSpec as P

STEP = 32
CORES = 2
LANES = 2
FIELD = 5
VMEM_BYTES = 32 * 1024 * 1024
SMEM_SPEC = pl.BlockSpec(memory_space=pltpu.SMEM)
VMEM_SPEC = pl.BlockSpec(memory_space=pltpu.VMEM)

OWN, OTHER = range(CORES)


def chip_slot(chip):
    return (chip & 3) * 4 + ((chip >> 2) & 1) * 2 + (chip >> 3)


def kernel_params():
    return pltpu.CompilerParams(vmem_limit_bytes=VMEM_BYTES)


def copies_body(block_ref, out_ref):
    block = block_ref[...]
    for i in range(out_ref.shape[0]):
        out_ref[i] = block


def copies_of(block, count):
    return pl.pallas_call(
        copies_body,
        out_shape=jax.ShapeDtypeStruct((count,) + block.shape, block.dtype),
        in_specs=[VMEM_SPEC],
        out_specs=VMEM_SPEC,
        compiler_params=kernel_params(),
    )(block)


def plan_body(chips, depth, here_ref, row_ref, col_ref, count_ref, tile_ref, order_ref, bound_ref, out_ref):
    slots, side, _ = tile_ref.shape
    positions = lax.broadcasted_iota(jnp.int32, (side, side), 0) * side + lax.broadcasted_iota(
        jnp.int32, (side, side), 1
    )

    def mask(i, carry):
        for u in range(8):
            k = i * 8 + u
            tile = tile_ref[k]
            out_ref[k] = jnp.where(positions < count_ref[k], tile, jnp.zeros_like(tile))
        return carry

    lax.fori_loop(0, slots // 8, mask, 0)
    out_ref[slots] = jnp.zeros((side, side), out_ref.dtype)

    def place(k):
        row, col = row_ref[k], col_ref[k]
        kind = lax.rem(row, CORES) ^ here_ref[0]
        chip = chip_slot(lax.div(row, CORES))
        lane = lax.div(col, depth)
        level = lax.rem(col, depth)
        turned = (lane * 2 + lax.rem(level, 2)) * (depth // 2) + lax.div(level, 2)
        return kind, k + ((chip + ((col + (turned << FIELD)) << FIELD)) << 8)

    zero = jnp.int32(0)
    others = lax.fori_loop(0, slots, lambda k, n: n + place(k)[0], zero)
    bound_ref[OWN] = zero
    bound_ref[OTHER] = slots - others
    bound_ref[CORES] = jnp.int32(slots)

    def put(k, nexts):
        kind, code = place(k)
        order_ref[jnp.where(kind == OWN, nexts[OWN], nexts[OTHER])] = code
        return nexts[OWN] + (1 - kind), nexts[OTHER] + kind

    lax.fori_loop(0, slots, put, (zero, slots - others))


def plan(here, rows, cols, counts, tiles, chips, depth):
    slots, side, _ = tiles.shape
    return pl.pallas_call(
        functools.partial(plan_body, chips, depth),
        out_shape=(
            jax.ShapeDtypeStruct((slots,), jnp.int32),
            jax.ShapeDtypeStruct((CORES + 1,), jnp.int32),
            jax.ShapeDtypeStruct((slots + 1, side, side), tiles.dtype),
        ),
        in_specs=[SMEM_SPEC] * 4 + [VMEM_SPEC],
        out_specs=(SMEM_SPEC, SMEM_SPEC, VMEM_SPEC),
        compiler_params=kernel_params(),
        cost_estimate=pl.CostEstimate(
            flops=tiles.size, bytes_accessed=4 * tiles.size, transcendentals=0
        ),
    )(here, rows, cols, counts, tiles)


def add_products(kind, forward, order_ref, bound_ref, tile_ref, block_ref, sum_ref):
    start, end = bound_ref[kind], bound_ref[kind + 1]
    slots = order_ref.shape[0]
    empty = tile_ref.shape[0] - 1

    def step(i, carry):
        for u in range(STEP):
            at = start + i * STEP + u
            code = jnp.where(at < end, order_ref[jnp.minimum(at, slots - 1)], empty)
            tile = tile_ref[code & 255]
            chip = (code >> 8) & ((1 << FIELD) - 1)
            if forward:
                level = (code >> (8 + FIELD)) & ((1 << FIELD) - 1)
                sum_ref[chip] += jnp.dot(
                    tile, block_ref[level], preferred_element_type=jnp.float32
                )
            else:
                turned = code >> (8 + 2 * FIELD)
                sum_ref[turned] += jnp.dot(
                    block_ref[chip], tile, preferred_element_type=jnp.float32
                )
        return carry

    lax.fori_loop(0, lax.div(end - start + (STEP - 1), STEP), step, 0)


def leaving_body(order_ref, bound_ref, tile_ref, block_ref, out_ref, total_ref):
    total_ref[...] = jnp.zeros_like(total_ref)
    add_products(OTHER, True, order_ref, bound_ref, tile_ref, block_ref, total_ref)
    out_ref[...] = total_ref[...].astype(out_ref.dtype)


def staying_body(order_ref, bound_ref, tile_ref, block_ref, total_ref):
    total_ref[...] = jnp.zeros_like(total_ref)
    add_products(OWN, True, order_ref, bound_ref, tile_ref, block_ref, total_ref)


def own_rows_body(order_ref, bound_ref, tile_ref, block_ref, sum_ref):
    sum_ref[...] = jnp.zeros_like(sum_ref)
    add_products(OWN, False, order_ref, bound_ref, tile_ref, block_ref, sum_ref)


def other_rows_body(order_ref, bound_ref, tile_ref, block_ref, sum_ref, out_ref, total_ref):
    total_ref[...] = sum_ref[...]
    add_products(OTHER, False, order_ref, bound_ref, tile_ref, block_ref, total_ref)
    out_ref[...] = total_ref[...].astype(out_ref.dtype)


def tile_products(body, tiles, blocks, sums, out_shapes, scratch, cost):
    order, bound, values = tiles
    operands = (order, bound, values, blocks) + sums
    return pl.pallas_call(
        body,
        out_shape=out_shapes,
        in_specs=[SMEM_SPEC] * 2 + [VMEM_SPEC] * (len(operands) - 2),
        out_specs=(VMEM_SPEC,) * len(out_shapes),
        scratch_shapes=scratch,
        compiler_params=kernel_params(),
        cost_estimate=pl.CostEstimate(flops=cost, bytes_accessed=cost // 128, transcendentals=0),
    )(*operands)


def stack_of(count, side, width, kind):
    return jax.ShapeDtypeStruct((count, side, width), kind)


def forward_sums(tiles, blocks, swap, chips):
    side, width = blocks.shape[1:]
    full = stack_of(chips, side, width, jnp.float32)
    half = stack_of(chips, side, width, jnp.bfloat16)
    cost = tiles[2].size * width
    total = (pltpu.VMEM(full.shape, jnp.float32),)
    (leaving,) = tile_products(leaving_body, tiles, blocks, (), (half,), total, cost)
    met = swap(leaving)
    (own,) = tile_products(staying_body, tiles, blocks, (), (full,), (), cost)
    return (own + met.astype(jnp.float32)).astype(jnp.bfloat16)


def backward_sums(tiles, near, send, square, members):
    width, side = near.shape[1:]
    full = stack_of(members, width, side, jnp.float32)
    half = stack_of(members, width, side, jnp.bfloat16)
    cost = tiles[2].size * width
    far = send(near)
    (own,) = tile_products(own_rows_body, tiles, near, (), (full,), (), cost)
    total = (pltpu.VMEM(full.shape, jnp.float32),)
    (sums,) = tile_products(other_rows_body, tiles, far, (own,), (half,), total, cost)
    met = square(sums).reshape(2 * LANES, -1, width, side).astype(jnp.float32)
    return (met[0] + met[1] + met[2] + met[3]).astype(jnp.bfloat16)


def dense_body(
    feature_ref, part_ref, cotangent_ref, self_ref, neigh_ref, activated_ref, copies_ref, own_ref
):
    aggregate = part_ref[0].astype(jnp.float32)
    for i in range(1, part_ref.shape[0]):
        aggregate += part_ref[i].astype(jnp.float32)
    preact = jnp.dot(
        feature_ref[...], self_ref[...], preferred_element_type=jnp.float32
    ) + jnp.dot(
        aggregate.astype(jnp.bfloat16), neigh_ref[...], preferred_element_type=jnp.float32
    )
    sigmoid_pre = 1.0 / (1.0 + jnp.exp(-preact))
    activated_ref[...] = (preact * sigmoid_pre).astype(jnp.bfloat16)
    derivative = sigmoid_pre * (1.0 + preact * (1.0 - sigmoid_pre))
    pre_grad = (cotangent_ref[...].astype(jnp.float32) * derivative).astype(jnp.bfloat16)
    across = (((1,), (1,)), ((), ()))
    neighbor = lax.dot_general(
        neigh_ref[...], pre_grad, across, preferred_element_type=jnp.float32
    ).astype(jnp.bfloat16)
    for i in range(copies_ref.shape[0]):
        copies_ref[i] = neighbor
    own_ref[...] = lax.dot_general(
        self_ref[...], pre_grad, across, preferred_element_type=jnp.float32
    )


def dense(features, parts, cotangent, w_self, w_neigh):
    rows, width = features.shape
    return pl.pallas_call(
        dense_body,
        out_shape=(
            jax.ShapeDtypeStruct(cotangent.shape, jnp.bfloat16),
            jax.ShapeDtypeStruct((parts.shape[0], width, rows), jnp.bfloat16),
            jax.ShapeDtypeStruct((width, rows), jnp.float32),
        ),
        compiler_params=kernel_params(),
    )(features, parts, cotangent, w_self, w_neigh)


def finish_body(own_ref, part_ref, out_ref):
    total = own_ref[...]
    for i in range(part_ref.shape[0]):
        total += part_ref[i].astype(jnp.float32)
    out_ref[...] = total.T.astype(jnp.bfloat16)


def finish(own, parts):
    width, rows = own.shape
    return pl.pallas_call(
        finish_body,
        out_shape=jax.ShapeDtypeStruct((rows, width), jnp.bfloat16),
        compiler_params=kernel_params(),
    )(own, parts)


def on_device(features, w_self, w_neigh, cotangent, tile_values, tile_row, tile_col, tile_count):
    teams = lax.axis_size("blk")
    members = lax.axis_size("rep")
    chips = teams // CORES
    depth = members // LANES
    same_core = [[chip * CORES + c for chip in sorted(range(chips), key=chip_slot)] for c in range(CORES)]
    same_lane = [[lane * depth + z for z in range(depth)] for lane in range(LANES)]
    same_parity = [
        [lane * depth + z for z in range(parity, depth, 2)]
        for lane in range(LANES)
        for parity in range(2)
    ]
    squares = [
        [lane * depth + z + parity for lane in range(LANES) for parity in range(2)]
        for z in range(0, depth, 2)
    ]
    to_other_core = [(i, i ^ 1) for i in range(teams)]
    same_level = [[lane * depth + z for lane in range(LANES)] for z in range(depth)]

    def between_chips(blocks):
        return lax.all_to_all(blocks, "blk", 0, 0, axis_index_groups=same_core, tiled=True)

    def along_depth(blocks):
        return lax.all_to_all(blocks, "rep", 0, 0, axis_index_groups=same_lane, tiled=True)

    def swap_cores(blocks):
        return lax.ppermute(blocks, "blk", to_other_core)

    def in_square(blocks):
        return lax.all_to_all(blocks, "rep", 0, 0, axis_index_groups=squares, tiled=True)

    def along_parity(blocks):
        return lax.all_to_all(blocks, "rep", 0, 0, axis_index_groups=same_parity, tiled=True)

    here = (lax.axis_index("blk") % CORES).astype(jnp.int32).reshape(1)
    tiles = plan(
        here, tile_row[0, 0], tile_col[0, 0], tile_count[0, 0], tile_values[0, 0], chips, depth
    )
    lane_rows = along_depth(copies_of(features, depth))
    lane_rows, tiles = lax.optimization_barrier((lane_rows, tiles))
    team_rows = lax.all_gather(
        lane_rows, "rep", axis=0, tiled=True, axis_index_groups=same_level
    )
    chip_sums = forward_sums(tiles, team_rows, swap_cores, chips)
    activated, copies, own_grad = dense(
        features, between_chips(chip_sums), cotangent, w_self, w_neigh
    )
    held = between_chips(copies)
    lane_terms = backward_sums(tiles, held, swap_cores, in_square, members)
    input_grad = finish(own_grad, along_parity(lane_terms))
    return activated, input_grad


def solution(mesh):
    placed = (
        P(("blk", "rep"), None),
        P(),
        P(),
        P(("blk", "rep"), None),
        P("blk", "rep", None, None, None),
        P("blk", "rep", None),
        P("blk", "rep", None),
        P("blk", "rep", None),
    )
    return jax.shard_map(
        on_device,
        mesh=mesh,
        in_specs=placed,
        out_specs=(P(("blk", "rep"), None), P(("blk", "rep"), None)),
        check_vma=False,
    )
```

```python
import functools

import jax
import jax.numpy as jnp
from jax import lax
from jax.experimental import pallas as pl
from jax.experimental.pallas import tpu as pltpu
from jax.sharding import PartitionSpec as P

STEP = 32
CORES = 2
LANES = 2
FIELD = 5
VMEM_BYTES = 32 * 1024 * 1024
SMEM_SPEC = pl.BlockSpec(memory_space=pltpu.SMEM)
VMEM_SPEC = pl.BlockSpec(memory_space=pltpu.VMEM)

OWN, OTHER = range(CORES)


def chip_slot(chip):
    x = (chip & 1) * 2 + ((chip >> 1) & 1)
    return x * 4 + ((chip >> 2) & 1) * 2 + (chip >> 3)


def kernel_params():
    return pltpu.CompilerParams(vmem_limit_bytes=VMEM_BYTES)


def copies_body(block_ref, out_ref):
    block = block_ref[...]
    for i in range(out_ref.shape[0]):
        out_ref[i] = block


def copies_of(block, count):
    return pl.pallas_call(
        copies_body,
        out_shape=jax.ShapeDtypeStruct((count,) + block.shape, block.dtype),
        in_specs=[VMEM_SPEC],
        out_specs=VMEM_SPEC,
        compiler_params=kernel_params(),
    )(block)


def plan_body(chips, depth, here_ref, row_ref, col_ref, count_ref, tile_ref, order_ref, bound_ref, out_ref):
    slots, side, _ = tile_ref.shape
    positions = lax.broadcasted_iota(jnp.int32, (side, side), 0) * side + lax.broadcasted_iota(
        jnp.int32, (side, side), 1
    )

    def mask(i, carry):
        for u in range(8):
            k = i * 8 + u
            tile = tile_ref[k]
            out_ref[k] = jnp.where(positions < count_ref[k], tile, jnp.zeros_like(tile))
        return carry

    lax.fori_loop(0, slots // 8, mask, 0)
    out_ref[slots] = jnp.zeros((side, side), out_ref.dtype)

    def place(k):
        row, col = row_ref[k], col_ref[k]
        kind = lax.rem(row, CORES) ^ here_ref[0]
        chip = chip_slot(lax.div(row, CORES))
        lane = lax.div(col, depth)
        level = lax.rem(col, depth)
        turned = (lane * 2 + lax.rem(level, 2)) * (depth // 2) + lax.div(level, 2)
        return kind, k + ((chip + ((col + (turned << FIELD)) << FIELD)) << 8)

    zero = jnp.int32(0)
    others = lax.fori_loop(0, slots, lambda k, n: n + place(k)[0], zero)
    bound_ref[OWN] = zero
    bound_ref[OTHER] = slots - others
    bound_ref[CORES] = jnp.int32(slots)

    def put(k, nexts):
        kind, code = place(k)
        order_ref[jnp.where(kind == OWN, nexts[OWN], nexts[OTHER])] = code
        return nexts[OWN] + (1 - kind), nexts[OTHER] + kind

    lax.fori_loop(0, slots, put, (zero, slots - others))


def plan(here, rows, cols, counts, tiles, chips, depth):
    slots, side, _ = tiles.shape
    return pl.pallas_call(
        functools.partial(plan_body, chips, depth),
        out_shape=(
            jax.ShapeDtypeStruct((slots,), jnp.int32),
            jax.ShapeDtypeStruct((CORES + 1,), jnp.int32),
            jax.ShapeDtypeStruct((slots + 1, side, side), tiles.dtype),
        ),
        in_specs=[SMEM_SPEC] * 4 + [VMEM_SPEC],
        out_specs=(SMEM_SPEC, SMEM_SPEC, VMEM_SPEC),
        compiler_params=kernel_params(),
        cost_estimate=pl.CostEstimate(
            flops=tiles.size, bytes_accessed=4 * tiles.size, transcendentals=0
        ),
    )(here, rows, cols, counts, tiles)


def add_products(kind, forward, order_ref, bound_ref, tile_ref, block_ref, sum_ref):
    start, end = bound_ref[kind], bound_ref[kind + 1]
    slots = order_ref.shape[0]
    empty = tile_ref.shape[0] - 1

    def step(i, carry):
        for u in range(STEP):
            at = start + i * STEP + u
            code = jnp.where(at < end, order_ref[jnp.minimum(at, slots - 1)], empty)
            tile = tile_ref[code & 255]
            chip = (code >> 8) & ((1 << FIELD) - 1)
            if forward:
                level = (code >> (8 + FIELD)) & ((1 << FIELD) - 1)
                sum_ref[chip] += jnp.dot(
                    tile, block_ref[level], preferred_element_type=jnp.float32
                )
            else:
                turned = code >> (8 + 2 * FIELD)
                sum_ref[turned] += jnp.dot(
                    block_ref[chip], tile, preferred_element_type=jnp.float32
                )
        return carry

    lax.fori_loop(0, lax.div(end - start + (STEP - 1), STEP), step, 0)


def leaving_body(order_ref, bound_ref, tile_ref, block_ref, out_ref, total_ref):
    total_ref[...] = jnp.zeros_like(total_ref)
    add_products(OTHER, True, order_ref, bound_ref, tile_ref, block_ref, total_ref)
    out_ref[...] = total_ref[...].astype(out_ref.dtype)


def staying_body(order_ref, bound_ref, tile_ref, block_ref, total_ref):
    total_ref[...] = jnp.zeros_like(total_ref)
    add_products(OWN, True, order_ref, bound_ref, tile_ref, block_ref, total_ref)


def own_rows_body(order_ref, bound_ref, tile_ref, block_ref, sum_ref):
    sum_ref[...] = jnp.zeros_like(sum_ref)
    add_products(OWN, False, order_ref, bound_ref, tile_ref, block_ref, sum_ref)


def other_rows_body(order_ref, bound_ref, tile_ref, block_ref, sum_ref, out_ref, total_ref):
    total_ref[...] = sum_ref[...]
    add_products(OTHER, False, order_ref, bound_ref, tile_ref, block_ref, total_ref)
    out_ref[...] = total_ref[...].astype(out_ref.dtype)


def tile_products(body, tiles, blocks, sums, out_shapes, scratch, cost):
    order, bound, values = tiles
    operands = (order, bound, values, blocks) + sums
    return pl.pallas_call(
        body,
        out_shape=out_shapes,
        in_specs=[SMEM_SPEC] * 2 + [VMEM_SPEC] * (len(operands) - 2),
        out_specs=(VMEM_SPEC,) * len(out_shapes),
        scratch_shapes=scratch,
        compiler_params=kernel_params(),
        cost_estimate=pl.CostEstimate(flops=cost, bytes_accessed=cost // 128, transcendentals=0),
    )(*operands)


def stack_of(count, side, width, kind):
    return jax.ShapeDtypeStruct((count, side, width), kind)


def forward_sums(tiles, blocks, swap, chips):
    side, width = blocks.shape[1:]
    full = stack_of(chips, side, width, jnp.float32)
    half = stack_of(chips, side, width, jnp.bfloat16)
    cost = tiles[2].size * width
    total = (pltpu.VMEM(full.shape, jnp.float32),)
    (leaving,) = tile_products(leaving_body, tiles, blocks, (), (half,), total, cost)
    met = swap(leaving)
    (own,) = tile_products(staying_body, tiles, blocks, (), (full,), (), cost)
    return (own + met.astype(jnp.float32)).astype(jnp.bfloat16)


def backward_sums(tiles, near, send, square, members):
    width, side = near.shape[1:]
    full = stack_of(members, width, side, jnp.float32)
    half = stack_of(members, width, side, jnp.bfloat16)
    cost = tiles[2].size * width
    far = send(near)
    (own,) = tile_products(own_rows_body, tiles, near, (), (full,), (), cost)
    total = (pltpu.VMEM(full.shape, jnp.float32),)
    (sums,) = tile_products(other_rows_body, tiles, far, (own,), (half,), total, cost)
    met = square(sums).reshape(2 * LANES, -1, width, side).astype(jnp.float32)
    return (met[0] + met[1] + met[2] + met[3]).astype(jnp.bfloat16)


def dense_body(
    feature_ref, part_ref, cotangent_ref, self_ref, neigh_ref, activated_ref, copies_ref, own_ref
):
    aggregate = part_ref[0].astype(jnp.float32)
    for i in range(1, part_ref.shape[0]):
        aggregate += part_ref[i].astype(jnp.float32)
    preact = jnp.dot(
        feature_ref[...], self_ref[...], preferred_element_type=jnp.float32
    ) + jnp.dot(
        aggregate.astype(jnp.bfloat16), neigh_ref[...], preferred_element_type=jnp.float32
    )
    sigmoid_pre = 1.0 / (1.0 + jnp.exp(-preact))
    activated_ref[...] = (preact * sigmoid_pre).astype(jnp.bfloat16)
    derivative = sigmoid_pre * (1.0 + preact * (1.0 - sigmoid_pre))
    pre_grad = (cotangent_ref[...].astype(jnp.float32) * derivative).astype(jnp.bfloat16)
    across = (((1,), (1,)), ((), ()))
    neighbor = lax.dot_general(
        neigh_ref[...], pre_grad, across, preferred_element_type=jnp.float32
    ).astype(jnp.bfloat16)
    for i in range(copies_ref.shape[0]):
        copies_ref[i] = neighbor
    own_ref[...] = lax.dot_general(
        self_ref[...], pre_grad, across, preferred_element_type=jnp.float32
    )


def dense(features, parts, cotangent, w_self, w_neigh):
    rows, width = features.shape
    return pl.pallas_call(
        dense_body,
        out_shape=(
            jax.ShapeDtypeStruct(cotangent.shape, jnp.bfloat16),
            jax.ShapeDtypeStruct((parts.shape[0], width, rows), jnp.bfloat16),
            jax.ShapeDtypeStruct((width, rows), jnp.float32),
        ),
        compiler_params=kernel_params(),
    )(features, parts, cotangent, w_self, w_neigh)


def finish_body(own_ref, part_ref, out_ref):
    total = own_ref[...]
    for i in range(part_ref.shape[0]):
        total += part_ref[i].astype(jnp.float32)
    out_ref[...] = total.T.astype(jnp.bfloat16)


def finish(own, parts):
    width, rows = own.shape
    return pl.pallas_call(
        finish_body,
        out_shape=jax.ShapeDtypeStruct((rows, width), jnp.bfloat16),
        compiler_params=kernel_params(),
    )(own, parts)


def on_device(features, w_self, w_neigh, cotangent, tile_values, tile_row, tile_col, tile_count):
    teams = lax.axis_size("blk")
    members = lax.axis_size("rep")
    chips = teams // CORES
    depth = members // LANES
    same_core = [[chip * CORES + c for chip in sorted(range(chips), key=chip_slot)] for c in range(CORES)]
    same_lane = [[lane * depth + z for z in range(depth)] for lane in range(LANES)]
    same_parity = [
        [lane * depth + z for z in range(parity, depth, 2)]
        for lane in range(LANES)
        for parity in range(2)
    ]
    squares = [
        [lane * depth + z + parity for lane in range(LANES) for parity in range(2)]
        for z in range(0, depth, 2)
    ]
    to_other_core = [(i, i ^ 1) for i in range(teams)]
    same_level = [[lane * depth + z for lane in range(LANES)] for z in range(depth)]

    def between_chips(blocks):
        return lax.all_to_all(blocks, "blk", 0, 0, axis_index_groups=same_core, tiled=True)

    def along_depth(blocks):
        return lax.all_to_all(blocks, "rep", 0, 0, axis_index_groups=same_lane, tiled=True)

    def swap_cores(blocks):
        return lax.ppermute(blocks, "blk", to_other_core)

    def in_square(blocks):
        return lax.all_to_all(blocks, "rep", 0, 0, axis_index_groups=squares, tiled=True)

    def along_parity(blocks):
        return lax.all_to_all(blocks, "rep", 0, 0, axis_index_groups=same_parity, tiled=True)

    here = (lax.axis_index("blk") % CORES).astype(jnp.int32).reshape(1)
    tiles = plan(
        here, tile_row[0, 0], tile_col[0, 0], tile_count[0, 0], tile_values[0, 0], chips, depth
    )
    lane_rows = along_depth(copies_of(features, depth))
    lane_rows, tiles = lax.optimization_barrier((lane_rows, tiles))
    team_rows = lax.all_gather(
        lane_rows, "rep", axis=0, tiled=True, axis_index_groups=same_level
    )
    chip_sums = forward_sums(tiles, team_rows, swap_cores, chips)
    activated, copies, own_grad = dense(
        features, between_chips(chip_sums), cotangent, w_self, w_neigh
    )
    held = between_chips(copies)
    lane_terms = backward_sums(tiles, held, swap_cores, in_square, members)
    input_grad = finish(own_grad, along_parity(lane_terms))
    return activated, input_grad


def solution(mesh):
    placed = (
        P(("blk", "rep"), None),
        P(),
        P(),
        P(("blk", "rep"), None),
        P("blk", "rep", None, None, None),
        P("blk", "rep", None),
        P("blk", "rep", None),
        P("blk", "rep", None),
    )
    return jax.shard_map(
        on_device,
        mesh=mesh,
        in_specs=placed,
        out_specs=(P(("blk", "rep"), None), P(("blk", "rep"), None)),
        check_vma=False,
    )
```
